256 devices in a mesh: row: 16 (over x_lo, y, core), col: 16 (over z, x_hi).
Axes of the slice: x: 4 (x_hi: 2, x_lo: 2; x = x_hi * 2 + x_lo), y: 4, z: 8, core: 2. Of those that a mesh axis runs over, the one named last changes fastest.
Arguments:
- inputs: bfloat16 [640, 12288], P('col', 'row'), may hold values from -6 to 6
- w_first: bfloat16 [12288, 49152], P('row', 'col'), may hold values from -0.0546875 to 0.0546875
- w_second: bfloat16 [49152, 12288], P('col', 'row'), may hold values from -0.02734375 to 0.02734375
- grad_out: bfloat16 [640, 12288], P('col', 'row'), may hold values from -6 to 6
Outputs:
- outputs: float32 [640, 12288], P('col', 'row')
- grad_in: float32 [640, 12288], P('col', 'row')
The draws below stay inside these ranges and needn't reach their ends.
All inputs are finite; a program needn't handle non-finite values.
Results may differ from the reference program's by a relative error of at most 0.0029.
Values may be sent and summed in bfloat16 or wider, within the bound.
A program may use at most 128 MiB of HBM per device.

```python
import jax
import jax.numpy as jnp
from jax import lax

D = 12288
FF = 49152
TOKENS = 640


def spiked(drawn, own_key, source, target, blocks, factor):
    def block_of(axis_at):
        return (jnp.arange(drawn.shape[axis_at]) // (drawn.shape[axis_at] // blocks)).reshape((-1,) + (1,) * (drawn.ndim - 1 - axis_at))

    first = jax.random.permutation(own_key, blocks)[block_of(target)]
    far = (block_of(target) + blocks // 2) % blocks
    return jnp.where((block_of(source) == first) | (block_of(source) == far), factor * drawn, drawn)


def shard_levels(rng, shape, pieces, least, top_value):
    factor_of, own = 1.0, jax.random.fold_in(rng, 6)
    for dim, shards_of in pieces:
        heights = jnp.exp(jax.random.uniform(jax.random.fold_in(own, dim), (shards_of,), jnp.float32, least / len(pieces), top_value / len(pieces)))
        factor_of = factor_of * jnp.repeat(heights, shape[dim] // shards_of).reshape([-1 if axis == dim else 1 for axis in range(len(shape))])
    return factor_of


def bell_draw(key, dims, spread, most, shards=(), dtype=jnp.bfloat16):
    loudness = shard_levels(key, dims, shards, -0.22, 0.18) if shards else 1.0
    drawn = jax.random.normal(key, dims, jnp.float32) * spread * loudness
    return jnp.minimum(jnp.maximum(drawn, -most), most).astype(dtype)


def noise_with(rng, dims, scale, limit, split, heavy, dtype=jnp.bfloat16):
    entries = scale * jax.random.normal(rng, dims, jnp.float32)
    if split:
        entries = entries * shard_levels(rng, dims, split, -0.22, 0.18)
    return jnp.clip(spiked(entries, jax.random.fold_in(rng, 3), *heavy), -limit, limit).astype(dtype)


def setup_inputs(seed: int = 0) -> dict:
    key_list = jax.random.split(jax.random.key(seed), 5)
    return {
        "inputs": noise_with(key_list[0], (TOKENS, D), 1.0, 6.0, ((0, 16), (1, 16)), (1, 0, 16, 2.0)),
        "w_first": bell_draw(key_list[1], (D, FF), D ** -0.5, 0.0546875, ((0, 16), (1, 16))),
        "w_second": bell_draw(key_list[2], (FF, D), FF ** -0.5, 0.02734375, ((0, 16), (1, 16))),
        "grad_out": noise_with(key_list[3], (TOKENS, D), 1.0, 6.0, ((0, 16), (1, 16)), (1, 0, 16, 2.0)),
    }


coef_a = 0.7978845608
coef_b = 0.044715


def gelu_value(h):
    t = jnp.tanh(coef_a * (h + coef_b * h * h * h))
    return 0.5 * h * (1.0 + t)


def gelu_slope(h):
    t = jnp.tanh(coef_a * (h + coef_b * h * h * h))
    return 0.5 * (1.0 + t) + 0.5 * h * (1.0 - t * t) * coef_a * (1.0 + 3.0 * coef_b * h * h)


def reference(inputs, w_first, w_second, grad_out):
    hidden = jnp.dot(inputs, w_first, preferred_element_type=jnp.float32)
    activated = gelu_value(hidden).astype(jnp.bfloat16)
    outputs = jnp.dot(activated, w_second, preferred_element_type=jnp.float32)
    grad_act = lax.dot_general(grad_out, w_second, (((1,), (1,)), ((), ())), preferred_element_type=jnp.float32)
    grad_hidden = (grad_act * gelu_slope(hidden)).astype(jnp.bfloat16)
    grad_in = lax.dot_general(grad_hidden, w_first, (((1,), (1,)), ((), ())), preferred_element_type=jnp.float32)
    return outputs, grad_in
```

```python
import functools

import jax
import jax.numpy as jnp
from jax import lax
from jax.experimental import pallas as pl
from jax.experimental.pallas import tpu as pltpu
from jax.sharding import PartitionSpec as P

MESH = pl.DeviceIdType.MESH
F32 = jnp.float32
BF16 = jnp.bfloat16

coef_a = 0.7978845608
coef_b = 0.044715

NY, NZ = 4, 8
LIFT = 2.0**19
DROP = 2.0**-19


def times(panel, weight):
    return jnp.dot(panel, weight, preferred_element_type=F32)


def times_transposed(panel, weight):
    return lax.dot_general(panel, weight, (((1,), (1,)), ((), ())), preferred_element_type=F32)


def coded(v):
    v = v * LIFT
    w = v * v
    w = w * w
    return jnp.where(v < 0, -w, w).astype(BF16)


def decoded(c):
    w = c.astype(F32)
    v = lax.rsqrt(lax.rsqrt(jnp.abs(w))) * DROP
    return jnp.where(w < 0, -v, v)


def kernel(
    T, inp, w1_hbm, w2_hbm, gout, out, gin,
    w1, w2, own, part, unit, sum_f, half_s, half_r, enc1, recv1h, recv1g, enc2h, enc2g, keep2h, keep2g,
    recv2h, recv2g, full, ob, orr, of, ot, mine, xs, xr,
    wsem, part_s, part_r, zp_s, zp_r, zm_s, zm_r, core_s, core_r, r1h_s, r1h_r, r1g_s, r1g_r,
    r2h_s, r2h_r, r2g_s, r2g_r, a1h_s, a1h_r, a1g_s, a1g_r, a2h_s, a2h_r, a2g_s, a2g_r,
    cs_s, cs_r, zo_s, zo_r, xo_s, xo_r,
):
    row = lax.axis_index("row")
    col = lax.axis_index("col")
    xl, y, core = row // 8, (row // 2) % NY, row % 2
    z, xh = col // 2, col % 2
    D = w1.shape[0]
    FF = w1.shape[1]
    HF = FF // 2
    QF = HF // NY
    M = 16 * NZ
    HM = M // 2

    def at_row(a, b, c):
        return (a * 8 + b * 2 + c, col)

    def at_col(a, b):
        return (row, a * 2 + b)

    dev_core = at_row(xl, y, 1 - core)
    dev_x = at_row(1 - xl, y, core)
    dev_y = [at_row(xl, (y + d) % NY, core) for d in range(1, NY)]
    dev_z = [at_col((z + d) % NZ, xh) for d in range(1, NZ)]
    dev_xh = at_col(z, 1 - xh)

    def remote(src, dst, ss, rs, dev):
        return pltpu.make_async_remote_copy(
            src_ref=src, dst_ref=dst, send_sem=ss, recv_sem=rs, device_id=dev, device_id_type=MESH
        )

    my_rows = pl.ds(pl.multiple_of(xl * HM, HM), HM)
    other_rows = pl.ds(pl.multiple_of((1 - xl) * HM, HM), HM)
    base = core * HF
    other_base = (1 - core) * HF

    def cols_of(q):
        return pl.ds(pl.multiple_of(q * QF, 128), QF)

    def full_cols_of(q):
        return pl.ds(pl.multiple_of(base + q * QF, 128), QF)

    my_half = pl.ds(pl.multiple_of(base, 128), HF)
    y_of = [(y + d) % NY for d in range(1, NY)]

    def c_part(k):
        return [remote(own.at[k], part.at[k], part_s.at[k], part_r.at[k], dev_xh)]

    def c_zplus(k, s):
        b = (z - s + NZ) % NZ
        rows = pl.ds(0, 16) if s == 3 else pl.ds(0, 32)
        ref = unit.at[k, b, rows, :]
        return remote(ref, ref, zp_s.at[k, s], zp_r.at[k, s], dev_z[0])

    def c_zminus(k, s):
        b = (z + s) % NZ
        rows = pl.ds(16, 16) if s == 3 else pl.ds(0, 32)
        ref = unit.at[k, b, rows, :]
        return remote(ref, ref, zm_s.at[k, s], zm_r.at[k, s], dev_z[NZ - 2])

    def c_core(k):
        return [remote(half_s.at[k], half_r.at[k], core_s.at[k], core_r.at[k], dev_core)]

    def c_rs1(k):
        got = [remote(enc1.at[k, 0, other_rows, :], recv1h.at[k], r1h_s.at[k], r1h_r.at[k], dev_x)]
        for d in (1, 0, 2):
            got.append(
                remote(
                    enc1.at[k, 1, :, cols_of(y_of[d])], recv1g.at[k, d], r1g_s.at[k, d], r1g_r.at[k, d], dev_y[d]
                )
            )
        return got

    def c_rs2(k):
        got = [remote(enc2g.at[k], recv2g.at[k], r2g_s.at[k], r2g_r.at[k], dev_x)]
        for d in (1, 0, 2):
            got.append(remote(enc2h.at[k, d], recv2h.at[k, d], r2h_s.at[k, d], r2h_r.at[k, d], dev_y[d]))
        return got

    def c_ag1(k):
        ref = full.at[k, 1, my_rows, full_cols_of(y)]
        got = [remote(ref, ref, a1g_s.at[k], a1g_r.at[k], dev_x)]
        ref = full.at[k, 0, my_rows, full_cols_of(y)]
        for d in (1, 0, 2):
            got.append(remote(ref, ref, a1h_s.at[k, d], a1h_r.at[k, d], dev_y[d]))
        return got

    def c_ag2(k):
        ref = full.at[k, 0, my_rows, my_half]
        got = [remote(ref, ref, a2h_s.at[k], a2h_r.at[k], dev_x)]
        ref = full.at[k, 1, :, full_cols_of(y)]
        for d in (1, 0, 2):
            got.append(remote(ref, ref, a2g_s.at[k, d], a2g_r.at[k, d], dev_y[d]))
        return got

    def c_share(k):
        ref = full.at[k, :, :, my_half]
        return [remote(ref, ref, cs_s.at[k], cs_r.at[k], dev_core)]

    def c_zout(k):
        got = []
        for d in (4, 3, 5, 2, 6, 1, 7):
            got.append(
                remote(
                    ob.at[k, (z + d) % NZ], orr.at[k, d - 1], zo_s.at[k, d - 1], zo_r.at[k, d - 1], dev_z[d - 1]
                )
            )
        return got

    def c_xout(k):
        return [remote(xs.at[k], xr.at[k], xo_s.at[k], xo_r.at[k], dev_xh)]

    def start(copies):
        for c in copies:
            c.start()

    def received(copies):
        for c in copies:
            c.wait_recv()

    def sent(copies):
        for c in copies:
            c.wait_send()

    def z_start(k):
        c_zplus(k, 0).start()
        c_zminus(k, 0).start()

    def z_step(k, s):
        c_zplus(k, s - 1).wait_recv()
        c_zplus(k, s).start()
        c_zminus(k, s - 1).wait_recv()
        c_zminus(k, s).start()

    def z_end(k):
        c_zplus(k, 3).wait_recv()
        c_zminus(k, 3).wait_recv()

    def build_unit(k):
        a = own[k].astype(F32)
        b = part[k].astype(F32)

        def joined(v, r):
            return jnp.concatenate([v[r : r + 8], v[r + 8 : r + 16]], axis=1)

        first = xh == 0
        pieces = []
        for r in (0, 16):
            m, o = joined(a, r), joined(b, r)
            pieces += [jnp.where(first, m, o), jnp.where(first, o, m)]
        unit[k, z] = jnp.concatenate(pieces, axis=0).astype(BF16)

    def first_products(k):
        xin = unit[k, :, 0:16, :].reshape(M, D)
        gin_ = unit[k, :, 16:32, :].reshape(M, D)
        step = 512
        for j in range(0, HF, step):
            at = pl.ds(pl.multiple_of(other_base + j, 128), step)
            half_s[k, 0, :, j : j + step] = times(xin, w1[:, at])
        for j in range(0, HF, step):
            at = pl.ds(pl.multiple_of(other_base + j, 128), step)
            half_s[k, 1, :, j : j + step] = times_transposed(gin_, w2[at, :])
        start(c_core(k))
        for j in range(0, HF, step):
            at = pl.ds(pl.multiple_of(base + j, 128), step)
            sum_f[k, 0, :, j : j + step] = times(xin, w1[:, at])
        for j in range(0, HF, step):
            at = pl.ds(pl.multiple_of(base + j, 128), step)
            sum_f[k, 1, :, j : j + step] = times_transposed(gin_, w2[at, :])

    def reduce_first(k):
        received(c_core(k))
        enc1[k, 0, other_rows, :] = coded(sum_f[k, 0, other_rows, :] + half_r[k, 0, other_rows, :])
        for d in range(NY - 1):
            at = cols_of(y_of[d])
            enc1[k, 1, :, at] = coded(sum_f[k, 1, :, at] + half_r[k, 1, :, at])
        start(c_rs1(k))
        sum_f[k, 0, my_rows, :] = sum_f[k, 0, my_rows, :] + half_r[k, 0, my_rows, :]
        at = cols_of(y)
        sum_f[k, 1, :, at] = sum_f[k, 1, :, at] + half_r[k, 1, :, at]

    def reduce_second(k):
        received(c_rs1(k))
        for d in range(NY - 1):
            at = cols_of(y_of[d])
            enc2h[k, d] = coded(sum_f[k, 0, my_rows, at] + decoded(recv1h[k, :, at]))
        at = cols_of(y)

        def total(rows):
            got = sum_f[k, 1, rows, at]
            for d in range(NY - 1):
                got = got + decoded(recv1g[k, d, rows, :])
            return got

        enc2g[k] = coded(total(other_rows))
        start(c_rs2(k))
        keep2h[k] = sum_f[k, 0, my_rows, at] + decoded(recv1h[k, :, at])
        keep2g[k] = total(my_rows)

    def activate(k):
        received(c_rs2(k))
        h = keep2h[k]
        for d in range(NY - 1):
            h = h + decoded(recv2h[k, d])
        g = keep2g[k] + decoded(recv2g[k])
        t = jnp.tanh(coef_a * (h + coef_b * h * h * h))
        act = 0.5 * h * (1.0 + t)
        slope = 0.5 * (1.0 + t) + 0.5 * h * (1.0 - t * t) * coef_a * (1.0 + 3.0 * coef_b * h * h)
        full[k, 0, my_rows, full_cols_of(y)] = act.astype(BF16)
        full[k, 1, my_rows, full_cols_of(y)] = (g * slope).astype(BF16)
        start(c_ag1(k))

    def gather_second(k):
        received(c_ag1(k))
        start(c_ag2(k))

    def gather_third(k):
        received(c_ag2(k))
        start(c_share(k))

    def second_products(k):
        received(c_share(k))
        o = times(full[k, 0], w2[...]).reshape(NZ, 16, D)
        ot[0] = o
        ob[k, :, 0:16, :] = o.astype(BF16)
        o = times_transposed(full[k, 1], w1[...]).reshape(NZ, 16, D)
        ot[1] = o
        ob[k, :, 16:32, :] = o.astype(BF16)
        start(c_zout(k))
        of[k] = ot[:, z]

    def reduce_out(k):
        received(c_zout(k))
        total = of[k].reshape(32, D)
        for d in range(NZ - 1):
            total = total + orr[k, d].astype(F32)
        first = xh == 0
        for i in range(2):
            lo, hi = total[16 * i : 16 * i + 8], total[16 * i + 8 : 16 * i + 16]
            mine[k, 8 * i : 8 * i + 8, :] = jnp.where(first, lo, hi)
            xs[k, 8 * i : 8 * i + 8, :] = jnp.where(first, hi, lo)
        start(c_xout(k))

    def finish(k):
        received(c_xout(k))
        at = pl.ds(pl.multiple_of(8 * k, 8), 8)
        out[at, :] = mine[k, 0:8, :] + xr[k, 0:8, :]
        gin[at, :] = mine[k, 8:16, :] + xr[k, 8:16, :]

    cw1 = pltpu.make_async_copy(w1_hbm, w1, wsem.at[0])
    cw2 = pltpu.make_async_copy(w2_hbm, w2, wsem.at[1])
    cw1.start()
    cw2.start()
    peers = [dev_core, dev_x, dev_xh] + dev_y + dev_z
    barrier = pltpu.get_barrier_semaphore()
    for p in peers:
        pl.semaphore_signal(barrier, inc=1, device_id=p, device_id_type=MESH)
    a = inp[...].astype(F32)
    g = gout[...].astype(F32)
    hd = D // 2
    for k in range(T):
        s = slice(8 * k, 8 * k + 8)
        own[k] = jnp.concatenate([a[s, :hd], a[s, hd:], g[s, :hd], g[s, hd:]], axis=0).astype(BF16)
    pl.semaphore_wait(barrier, len(peers))
    for k in range(T):
        start(c_part(k))
    received(c_part(0))
    build_unit(0)
    z_start(0)
    for s in range(1, T):
        received(c_part(s))
        build_unit(s)
    for s in range(1, 4):
        z_step(0, s)
    cw1.wait()
    cw2.wait()
    z_end(0)
    first_products(0)

    def step(t, carry):
        def when(k, body):
            @pl.when(jnp.logical_and(k >= 0, k < T))
            def _():
                body(k)

        when(t - 1, activate)
        when(t, reduce_first)
        when(t + 1, z_start)
        when(t - 2, gather_third)
        when(t + 1, lambda k: z_step(k, 1))
        when(t - 3, reduce_out)
        when(t - 2, second_products)
        when(t + 1, lambda k: z_step(k, 2))
        when(t - 1, gather_second)
        when(t, reduce_second)
        when(t + 1, lambda k: z_step(k, 3))
        when(t + 1, z_end)
        when(t + 1, first_products)
        when(t - 3, finish)
        return carry

    lax.fori_loop(0, T + 3, step, 0)

    def drain(k, carry):
        for copies in (c_part, c_core, c_rs1, c_rs2, c_ag1, c_ag2, c_share, c_zout, c_xout):
            sent(copies(k))
        for s in range(4):
            c_zplus(k, s).wait_send()
            c_zminus(k, s).wait_send()
        return carry

    lax.fori_loop(0, T, drain, 0)


def on_device(inputs, w_first, w_second, grad_out):
    tokens, D = inputs.shape
    FF = w_first.shape[1]
    T = tokens // 8
    M = 16 * NZ
    HM, HF = M // 2, FF // 2
    QF = HF // NY
    V = pl.BlockSpec(memory_space=pltpu.VMEM)
    ANY = pl.BlockSpec(memory_space=pl.ANY)
    shape = jax.ShapeDtypeStruct((tokens, D), F32)
    dma = pltpu.SemaphoreType.DMA
    one, three = dma((T,)), dma((T, NY - 1))
    buffers = [
        pltpu.VMEM((D, FF), BF16),
        pltpu.VMEM((FF, D), BF16),
        pltpu.VMEM((T, 32, D // 2), BF16),
        pltpu.VMEM((T, 32, D // 2), BF16),
        pltpu.VMEM((T, NZ, 32, D), BF16),
        pltpu.VMEM((T, 2, M, HF), F32),
        pltpu.VMEM((T, 2, M, HF), F32),
        pltpu.VMEM((T, 2, M, HF), F32),
        pltpu.VMEM((T, 2, M, HF), BF16),
        pltpu.VMEM((T, HM, HF), BF16),
        pltpu.VMEM((T, NY - 1, M, QF), BF16),
        pltpu.VMEM((T, NY - 1, HM, QF), BF16),
        pltpu.VMEM((T, HM, QF), BF16),
        pltpu.VMEM((T, HM, QF), F32),
        pltpu.VMEM((T, HM, QF), F32),
        pltpu.VMEM((T, NY - 1, HM, QF), BF16),
        pltpu.VMEM((T, HM, QF), BF16),
        pltpu.VMEM((T, 2, M, FF), BF16),
        pltpu.VMEM((T, NZ, 32, D), BF16),
        pltpu.VMEM((T, NZ - 1, 32, D), BF16),
        pltpu.VMEM((T, 2, 16, D), F32),
        pltpu.VMEM((2, NZ, 16, D), F32),
        pltpu.VMEM((T, 16, D), F32),
        pltpu.VMEM((T, 16, D), F32),
        pltpu.VMEM((T, 16, D), F32),
    ]
    semaphores = [
        dma((2,)),
        one, one,
        dma((T, 4)), dma((T, 4)), dma((T, 4)), dma((T, 4)),
        one, one,
        one, one, three, three,
        three, three, one, one,
        three, three, one, one,
        one, one, three, three,
        one, one,
        dma((T, NZ - 1)), dma((T, NZ - 1)),
        one, one,
    ]
    flops = 4 * 2 * M * T * D * FF
    return pl.pallas_call(
        functools.partial(kernel, T),
        out_shape=(shape, shape),
        in_specs=[V, ANY, ANY, V],
        out_specs=(V, V),
        scratch_shapes=buffers + semaphores,
        compiler_params=pltpu.CompilerParams(
            collective_id=0, has_side_effects=True, vmem_limit_bytes=63 * 2**20
        ),
        cost_estimate=pl.CostEstimate(flops=flops, bytes_accessed=4 * D * FF, transcendentals=0),
    )(inputs, w_first, w_second, grad_out)


def solution(mesh):
    in_specs = (P("col", "row"), P("row", "col"), P("col", "row"), P("col", "row"))
    out_specs = (P("col", "row"), P("col", "row"))
    return jax.shard_map(
        on_device, mesh=mesh, in_specs=in_specs, out_specs=out_specs, check_vma=False
    )
```

```python
import functools

import jax
import jax.numpy as jnp
from jax import lax
from jax.experimental import pallas as pl
from jax.experimental.pallas import tpu as pltpu
from jax.sharding import PartitionSpec as P

MESH = pl.DeviceIdType.MESH
F32 = jnp.float32
BF16 = jnp.bfloat16

coef_a = 0.7978845608
coef_b = 0.044715

NY, NZ = 4, 8
NEAR = (3, 5, 2, 6, 1, 7)
LIFT = 2.0**19
LIFT_OUT = 2.0**8


def times(panel, weight):
    return jnp.dot(panel, weight, preferred_element_type=F32)


def times_transposed(panel, weight):
    return lax.dot_general(panel, weight, (((1,), (1,)), ((), ())), preferred_element_type=F32)


def coded(v, lift=LIFT):
    v = v * lift
    w = v * v
    w = w * w
    return jnp.where(v < 0, -w, w).astype(BF16)


def decoded(c, lift=LIFT):
    w = c.astype(F32)
    v = lax.rsqrt(lax.rsqrt(jnp.abs(w))) * (1.0 / lift)
    return jnp.where(w < 0, -v, v)


def kernel(
    T, inp, w1_hbm, w2_hbm, gout, out, gin,
    w1, w2, own, part, unit, sum_f, half_s, half_r, enc1, recv1h, recv1g, enc2h, enc2g, keep2h, keep2g,
    recv2h, recv2g, full, out_s, out_r, far_s, far_r, ot, mine, xs, xr,
    wsem, part_s, part_r, zn_s, zn_r, zf_s, zf_r, core_s, core_r, r1h_s, r1h_r, r1g_s, r1g_r,
    r2h_s, r2h_r, r2g_s, r2g_r, a1h_s, a1h_r, a1g_s, a1g_r, a2h_s, a2h_r, a2g_s, a2g_r,
    cs_s, cs_r, on_s, on_r, of_s, of_r, xo_s, xo_r,
):
    row = lax.axis_index("row")
    col = lax.axis_index("col")
    xl, y, core = row // 8, (row // 2) % NY, row % 2
    z, xh = col // 2, col % 2
    D = w1.shape[0]
    FF = w1.shape[1]
    HF = FF // 2
    QF = HF // NY
    M = 16 * NZ
    HM = M // 2

    def at_row(a, b, c):
        return (a * 8 + b * 2 + c, col)

    def at_col(a, b):
        return (row, a * 2 + b)

    dev_core = at_row(xl, y, 1 - core)
    dev_x = at_row(1 - xl, y, core)
    dev_y = [at_row(xl, (y + d) % NY, core) for d in range(1, NY)]
    dev_z = [at_col((z + d) % NZ, xh) for d in range(NZ)]
    dev_xh = at_col(z, 1 - xh)

    def remote(src, dst, ss, rs, dev):
        return pltpu.make_async_remote_copy(
            src_ref=src, dst_ref=dst, send_sem=ss, recv_sem=rs, device_id=dev, device_id_type=MESH
        )

    my_rows = pl.ds(pl.multiple_of(xl * HM, HM), HM)
    other_rows = pl.ds(pl.multiple_of((1 - xl) * HM, HM), HM)
    base = core * HF
    other_base = (1 - core) * HF

    def cols_of(q):
        return pl.ds(pl.multiple_of(q * QF, 128), QF)

    def full_cols_of(q):
        return pl.ds(pl.multiple_of(base + q * QF, 128), QF)

    my_half = pl.ds(pl.multiple_of(base, 128), HF)
    y_of = [(y + d) % NY for d in range(1, NY)]

    def c_part(k):
        return [remote(own.at[k], part.at[k], part_s.at[k], part_r.at[k], dev_xh)]

    def c_near(k, ds=NEAR):
        ref = unit.at[k, z]
        return [remote(ref, ref, zn_s.at[k, d - 1], zn_r.at[k, d - 1], dev_z[d]) for d in ds]

    def c_far(k):
        got = []
        for i, (b, d) in enumerate(((NZ - 3, 1), (3, NZ - 1))):
            ref = unit.at[k, (z + b) % NZ, pl.ds(16 * i, 16), :]
            got.append(remote(ref, ref, zf_s.at[k, i], zf_r.at[k, i], dev_z[d]))
        return got

    def c_core(k):
        return [remote(half_s.at[k], half_r.at[k], core_s.at[k], core_r.at[k], dev_core)]

    def c_rs1(k):
        got = [remote(enc1.at[k, 0, other_rows, :], recv1h.at[k], r1h_s.at[k], r1h_r.at[k], dev_x)]
        for d in (1, 0, 2):
            got.append(
                remote(
                    enc1.at[k, 1, :, cols_of(y_of[d])], recv1g.at[k, d], r1g_s.at[k, d], r1g_r.at[k, d], dev_y[d]
                )
            )
        return got

    def c_rs2(k):
        got = [remote(enc2g.at[k], recv2g.at[k], r2g_s.at[k], r2g_r.at[k], dev_x)]
        for d in (1, 0, 2):
            got.append(remote(enc2h.at[k, d], recv2h.at[k, d], r2h_s.at[k, d], r2h_r.at[k, d], dev_y[d]))
        return got

    def c_ag1(k):
        ref = full.at[k, 1, my_rows, full_cols_of(y)]
        got = [remote(ref, ref, a1g_s.at[k], a1g_r.at[k], dev_x)]
        ref = full.at[k, 0, my_rows, full_cols_of(y)]
        for d in (1, 0, 2):
            got.append(remote(ref, ref, a1h_s.at[k, d], a1h_r.at[k, d], dev_y[d]))
        return got

    def c_ag2(k):
        ref = full.at[k, 0, my_rows, my_half]
        got = [remote(ref, ref, a2h_s.at[k], a2h_r.at[k], dev_x)]
        ref = full.at[k, 1, :, full_cols_of(y)]
        for d in (1, 0, 2):
            got.append(remote(ref, ref, a2g_s.at[k, d], a2g_r.at[k, d], dev_y[d]))
        return got

    def c_share(k):
        ref = full.at[k, :, :, my_half]
        return [remote(ref, ref, cs_s.at[k], cs_r.at[k], dev_core)]

    def c_out(k, ds):
        return [
            remote(out_s.at[k, d - 1], out_r.at[k, d - 1], on_s.at[k, d - 1], on_r.at[k, d - 1], dev_z[d]) for d in ds
        ]

    def c_out_far(k):
        got = []
        for i, d in enumerate((1, NZ - 1)):
            rows = pl.ds(16 * i, 16)
            got.append(
                remote(far_s.at[k, rows, :], far_r.at[k, rows, :], of_s.at[k, i], of_r.at[k, i], dev_z[d])
            )
        return got

    def c_xout(k):
        return [remote(xs.at[k], xr.at[k], xo_s.at[k], xo_r.at[k], dev_xh)]

    def start(copies):
        for c in copies:
            c.start()

    def received(copies):
        for c in copies:
            c.wait_recv()

    def sent(copies):
        for c in copies:
            c.wait_send()

    def z_start(k):
        start(c_near(k))

    def z_pass(k):
        received(c_near(k, NEAR[:2]))
        start(c_far(k))

    def z_end(k):
        received(c_near(k, NEAR[2:]))
        received(c_far(k))

    def build_unit(k):
        a = own[k].astype(F32)
        b = part[k].astype(F32)

        def joined(v, r):
            return jnp.concatenate([v[r : r + 8], v[r + 8 : r + 16]], axis=1)

        first = xh == 0
        pieces = []
        for r in (0, 16):
            m, o = joined(a, r), joined(b, r)
            pieces += [jnp.where(first, m, o), jnp.where(first, o, m)]
        unit[k, z] = jnp.concatenate(pieces, axis=0).astype(BF16)

    def first_products(k):
        xin = unit[k, :, 0:16, :].reshape(M, D)
        gin_ = unit[k, :, 16:32, :].reshape(M, D)
        step = 512
        for j in range(0, HF, step):
            at = pl.ds(pl.multiple_of(other_base + j, 128), step)
            half_s[k, 0, :, j : j + step] = times(xin, w1[:, at])
        for j in range(0, HF, step):
            at = pl.ds(pl.multiple_of(other_base + j, 128), step)
            half_s[k, 1, :, j : j + step] = times_transposed(gin_, w2[at, :])
        start(c_core(k))
        for j in range(0, HF, step):
            at = pl.ds(pl.multiple_of(base + j, 128), step)
            sum_f[k, 0, :, j : j + step] = times(xin, w1[:, at])
        for j in range(0, HF, step):
            at = pl.ds(pl.multiple_of(base + j, 128), step)
            sum_f[k, 1, :, j : j + step] = times_transposed(gin_, w2[at, :])

    def reduce_first(k):
        received(c_core(k))
        enc1[k, 0, other_rows, :] = coded(sum_f[k, 0, other_rows, :] + half_r[k, 0, other_rows, :])
        for d in range(NY - 1):
            at = cols_of(y_of[d])
            enc1[k, 1, :, at] = coded(sum_f[k, 1, :, at] + half_r[k, 1, :, at])
        start(c_rs1(k))
        sum_f[k, 0, my_rows, :] = sum_f[k, 0, my_rows, :] + half_r[k, 0, my_rows, :]
        at = cols_of(y)
        sum_f[k, 1, :, at] = sum_f[k, 1, :, at] + half_r[k, 1, :, at]

    def reduce_second(k):
        received(c_rs1(k))
        for d in range(NY - 1):
            at = cols_of(y_of[d])
            enc2h[k, d] = coded(sum_f[k, 0, my_rows, at] + decoded(recv1h[k, :, at]))
        at = cols_of(y)

        def total(rows):
            got = sum_f[k, 1, rows, at]
            for d in range(NY - 1):
                got = got + decoded(recv1g[k, d, rows, :])
            return got

        enc2g[k] = coded(total(other_rows))
        start(c_rs2(k))
        keep2h[k] = sum_f[k, 0, my_rows, at] + decoded(recv1h[k, :, at])
        keep2g[k] = total(my_rows)

    def activate(k):
        received(c_rs2(k))
        h = keep2h[k]
        for d in range(NY - 1):
            h = h + decoded(recv2h[k, d])
        g = keep2g[k] + decoded(recv2g[k])
        t = jnp.tanh(coef_a * (h + coef_b * h * h * h))
        act = 0.5 * h * (1.0 + t)
        slope = 0.5 * (1.0 + t) + 0.5 * h * (1.0 - t * t) * coef_a * (1.0 + 3.0 * coef_b * h * h)
        full[k, 0, my_rows, full_cols_of(y)] = act.astype(BF16)
        full[k, 1, my_rows, full_cols_of(y)] = (g * slope).astype(BF16)
        start(c_ag1(k))

    def gather_second(k):
        received(c_ag1(k))
        start(c_ag2(k))

    def gather_third(k):
        received(c_ag2(k))
        start(c_share(k))

    def own_out(k, b):
        return ot[k % 3, :, b].reshape(32, D)

    def out_first(k):
        v = own_out(k, (z + 4) % NZ)
        far_s[k] = coded(v, LIFT_OUT)
        start(c_out_far(k))
        for d in (2, 6, 1, 7):
            out_s[k, d - 1] = coded(own_out(k, (z + d) % NZ), LIFT_OUT)
            start(c_out(k, (d,)))

    def out_second(k):
        c = c_out_far(k)
        c[0].wait_recv()
        v = own_out(k, (z + 3) % NZ)
        out_s[k, 2, 0:16, :] = coded(v[0:16] + decoded(far_r[k, 0:16, :], LIFT_OUT), LIFT_OUT)
        out_s[k, 2, 16:32, :] = coded(v[16:32], LIFT_OUT)
        start(c_out(k, (3,)))
        c[1].wait_recv()
        v = own_out(k, (z + 5) % NZ)
        out_s[k, 4, 0:16, :] = coded(v[0:16], LIFT_OUT)
        out_s[k, 4, 16:32, :] = coded(v[16:32] + decoded(far_r[k, 16:32, :], LIFT_OUT), LIFT_OUT)
        start(c_out(k, (5,)))

    def second_products(k):
        received(c_share(k))
        ot[k % 3, 0] = times(full[k, 0], w2[...]).reshape(NZ, 16, D)
        ot[k % 3, 1] = times_transposed(full[k, 1], w1[...]).reshape(NZ, 16, D)
        out_first(k)

    def reduce_out(k):
        received(c_out(k, NEAR))
        total = own_out(k, z)
        for d in NEAR:
            total = total + decoded(out_r[k, d - 1], LIFT_OUT)
        first = xh == 0
        for i in range(2):
            lo, hi = total[16 * i : 16 * i + 8], total[16 * i + 8 : 16 * i + 16]
            mine[k, 8 * i : 8 * i + 8, :] = jnp.where(first, lo, hi)
            xs[k, 8 * i : 8 * i + 8, :] = jnp.where(first, hi, lo)
        start(c_xout(k))

    def finish(k):
        received(c_xout(k))
        at = pl.ds(pl.multiple_of(8 * k, 8), 8)
        out[at, :] = mine[k, 0:8, :] + xr[k, 0:8, :]
        gin[at, :] = mine[k, 8:16, :] + xr[k, 8:16, :]

    cw1 = pltpu.make_async_copy(w1_hbm, w1, wsem.at[0])
    cw2 = pltpu.make_async_copy(w2_hbm, w2, wsem.at[1])
    cw1.start()
    cw2.start()
    peers = [dev_core, dev_x, dev_xh] + dev_y + [dev_z[d] for d in NEAR]
    barrier = pltpu.get_barrier_semaphore()
    for p in peers:
        pl.semaphore_signal(barrier, inc=1, device_id=p, device_id_type=MESH)
    a = inp[...].astype(F32)
    g = gout[...].astype(F32)
    hd = D // 2
    for k in range(T):
        s = slice(8 * k, 8 * k + 8)
        own[k] = jnp.concatenate([a[s, :hd], a[s, hd:], g[s, :hd], g[s, hd:]], axis=0).astype(BF16)
    pl.semaphore_wait(barrier, len(peers))
    for k in range(T):
        start(c_part(k))
    received(c_part(0))
    build_unit(0)
    z_start(0)
    for k in range(1, T):
        received(c_part(k))
        build_unit(k)
    z_pass(0)
    z_start(1)
    cw1.wait()
    cw2.wait()

    def step(t, carry):
        def when(k, body):
            @pl.when(jnp.logical_and(k >= 0, k < T))
            def _():
                body(k)

        when(t - 1, activate)
        when(t, reduce_second)
        when(t - 2, gather_second)
        when(t - 4, out_second)
        when(t + 1, reduce_first)
        when(t - 3, gather_third)
        when(t + 2, z_end)
        when(t + 2, first_products)
        when(t - 5, finish)
        when(t - 3, second_products)
        when(t - 4, reduce_out)

        @pl.when(jnp.logical_and(t + 3 >= 1, t + 3 < T))
        def _():
            z_pass(t + 3)

        @pl.when(jnp.logical_and(t + 4 >= 2, t + 4 < T))
        def _():
            z_start(t + 4)

        return carry

    lax.fori_loop(-2, T + 3, step, 0)

    def drain(k, carry):
        for copies in (c_part, c_core, c_rs1, c_rs2, c_ag1, c_ag2, c_share):
            sent(copies(k))
        sent(c_near(k))
        sent(c_far(k))
        return carry

    def drain_out(k, carry):
        sent(c_out_far(k))
        sent(c_out(k, NEAR))
        sent(c_xout(k))
        return carry

    last = T - 1
    out_second(last)
    finish(last - 1)
    lax.fori_loop(0, T, drain, 0)
    lax.fori_loop(0, last, drain_out, 0)
    reduce_out(last)
    finish(last)
    drain_out(last, 0)


def on_device(inputs, w_first, w_second, grad_out):
    tokens, D = inputs.shape
    FF = w_first.shape[1]
    T = tokens // 8
    M = 16 * NZ
    HM, HF = M // 2, FF // 2
    QF = HF // NY
    V = pl.BlockSpec(memory_space=pltpu.VMEM)
    ANY = pl.BlockSpec(memory_space=pl.ANY)
    shape = jax.ShapeDtypeStruct((tokens, D), F32)
    dma = pltpu.SemaphoreType.DMA
    one, three = dma((T,)), dma((T, NY - 1))
    buffers = [
        pltpu.VMEM((D, FF), BF16),
        pltpu.VMEM((FF, D), BF16),
        pltpu.VMEM((T, 32, D // 2), BF16),
        pltpu.VMEM((T, 32, D // 2), BF16),
        pltpu.VMEM((T, NZ, 32, D), BF16),
        pltpu.VMEM((T, 2, M, HF), F32),
        pltpu.VMEM((T, 2, M, HF), F32),
        pltpu.VMEM((T, 2, M, HF), F32),
        pltpu.VMEM((T, 2, M, HF), BF16),
        pltpu.VMEM((T, HM, HF), BF16),
        pltpu.VMEM((T, NY - 1, M, QF), BF16),
        pltpu.VMEM((T, NY - 1, HM, QF), BF16),
        pltpu.VMEM((T, HM, QF), BF16),
        pltpu.VMEM((T, HM, QF), F32),
        pltpu.VMEM((T, HM, QF), F32),
        pltpu.VMEM((T, NY - 1, HM, QF), BF16),
        pltpu.VMEM((T, HM, QF), BF16),
        pltpu.VMEM((T, 2, M, FF), BF16),
        pltpu.VMEM((T, NZ - 1, 32, D), BF16),
        pltpu.VMEM((T, NZ - 1, 32, D), BF16),
        pltpu.VMEM((T, 32, D), BF16),
        pltpu.VMEM((T, 32, D), BF16),
        pltpu.VMEM((3, 2, NZ, 16, D), F32),
        pltpu.VMEM((T, 16, D), F32),
        pltpu.VMEM((T, 16, D), F32),
        pltpu.VMEM((T, 16, D), F32),
    ]
    semaphores = [
        dma((2,)),
        one, one,
        dma((T, NZ - 1)), dma((T, NZ - 1)), dma((T, 2)), dma((T, 2)),
        one, one,
        one, one, three, three,
        three, three, one, one,
        three, three, one, one,
        one, one, three, three,
        one, one,
        dma((T, NZ - 1)), dma((T, NZ - 1)), dma((T, 2)), dma((T, 2)),
        one, one,
    ]
    flops = 4 * 2 * M * T * D * FF
    return pl.pallas_call(
        functools.partial(kernel, T),
        out_shape=(shape, shape),
        in_specs=[V, ANY, ANY, V],
        out_specs=(V, V),
        scratch_shapes=buffers + semaphores,
        compiler_params=pltpu.CompilerParams(
            collective_id=0, has_side_effects=True, vmem_limit_bytes=63 * 2**20
        ),
        cost_estimate=pl.CostEstimate(flops=flops, bytes_accessed=4 * D * FF, transcendentals=0),
    )(inputs, w_first, w_second, grad_out)


def solution(mesh):
    in_specs = (P("col", "row"), P("row", "col"), P("col", "row"), P("col", "row"))
    out_specs = (P("col", "row"), P("col", "row"))
    return jax.shard_map(
        on_device, mesh=mesh, in_specs=in_specs, out_specs=out_specs, check_vma=False
    )
```

```python
import functools

import jax
import jax.numpy as jnp
from jax import lax
from jax.experimental import pallas as pl
from jax.experimental.pallas import tpu as pltpu
from jax.sharding import PartitionSpec as P

MESH = pl.DeviceIdType.MESH
F32 = jnp.float32
BF16 = jnp.bfloat16

coef_a = 0.7978845608
coef_b = 0.044715

NY, NZ = 4, 8
NEAR = (3, 5, 2, 6, 1, 7)
LIFT = 2.0**19
LIFT_OUT = 2.0**8


def times(panel, weight):
    return jnp.dot(panel, weight, preferred_element_type=F32)


def times_transposed(panel, weight):
    return lax.dot_general(panel, weight, (((1,), (1,)), ((), ())), preferred_element_type=F32)


def coded(v, lift=LIFT):
    v = v * lift
    w = v * v
    w = w * w
    return jnp.where(v < 0, -w, w).astype(BF16)


def decoded(c, lift=LIFT):
    w = c.astype(F32)
    v = lax.rsqrt(lax.rsqrt(jnp.abs(w))) * (1.0 / lift)
    return jnp.where(w < 0, -v, v)


def kernel(
    T, inp, w1_hbm, w2_hbm, gout, out, gin,
    w1, w2, own, part, unit, sum_f, half_s, half_r, enc1, recv1h, recv1g, enc2h, enc2g, keep2h, keep2g,
    recv2h, recv2g, full, out_s, out_r, far_s, far_r, ot, mine, xs, xr,
    wsem, part_s, part_r, zn_s, zn_r, zf_s, zf_r, core_s, core_r, r1h_s, r1h_r, r1g_s, r1g_r,
    r2h_s, r2h_r, r2g_s, r2g_r, a1h_s, a1h_r, a1g_s, a1g_r, a2h_s, a2h_r, a2g_s, a2g_r,
    cs_s, cs_r, on_s, on_r, of_s, of_r, xo_s, xo_r,
):
    row = lax.axis_index("row")
    col = lax.axis_index("col")
    xl, y, core = row // 8, (row // 2) % NY, row % 2
    z, xh = col // 2, col % 2
    D = w1.shape[0]
    FF = w1.shape[1]
    HF = FF // 2
    QF = HF // NY
    M = 16 * NZ
    HM = M // 2

    def at_row(a, b, c):
        return (a * 8 + b * 2 + c, col)

    def at_col(a, b):
        return (row, a * 2 + b)

    dev_core = at_row(xl, y, 1 - core)
    dev_x = at_row(1 - xl, y, core)
    dev_y = [at_row(xl, (y + d) % NY, core) for d in range(1, NY)]
    dev_z = [at_col((z + d) % NZ, xh) for d in range(NZ)]
    dev_xh = at_col(z, 1 - xh)

    def remote(src, dst, ss, rs, dev):
        return pltpu.make_async_remote_copy(
            src_ref=src, dst_ref=dst, send_sem=ss, recv_sem=rs, device_id=dev, device_id_type=MESH
        )

    my_rows = pl.ds(pl.multiple_of(xl * HM, HM), HM)
    other_rows = pl.ds(pl.multiple_of((1 - xl) * HM, HM), HM)
    base = core * HF
    other_base = (1 - core) * HF

    def cols_of(q):
        return pl.ds(pl.multiple_of(q * QF, 128), QF)

    def full_cols_of(q):
        return pl.ds(pl.multiple_of(base + q * QF, 128), QF)

    my_half = pl.ds(pl.multiple_of(base, 128), HF)
    y_of = [(y + d) % NY for d in range(1, NY)]

    def c_part(k):
        return [remote(own.at[k], part.at[k], part_s.at[k], part_r.at[k], dev_xh)]

    def c_near(k, ds=NEAR):
        ref = unit.at[k, z]
        return [remote(ref, ref, zn_s.at[k, d - 1], zn_r.at[k, d - 1], dev_z[d]) for d in ds]

    def c_far(k):
        got = []
        for i, (b, d) in enumerate(((NZ - 3, 1), (3, NZ - 1))):
            ref = unit.at[k, (z + b) % NZ, pl.ds(16 * i, 16), :]
            got.append(remote(ref, ref, zf_s.at[k, i], zf_r.at[k, i], dev_z[d]))
        return got

    def c_core(k):
        return [remote(half_s.at[k], half_r.at[k], core_s.at[k], core_r.at[k], dev_core)]

    def c_rs1(k):
        got = [remote(enc1.at[k, 0, other_rows, :], recv1h.at[k], r1h_s.at[k], r1h_r.at[k], dev_x)]
        for d in (1, 0, 2):
            got.append(
                remote(
                    enc1.at[k, 1, :, cols_of(y_of[d])], recv1g.at[k, d], r1g_s.at[k, d], r1g_r.at[k, d], dev_y[d]
                )
            )
        return got

    def c_rs2(k):
        got = [remote(enc2g.at[k], recv2g.at[k], r2g_s.at[k], r2g_r.at[k], dev_x)]
        for d in (1, 0, 2):
            got.append(remote(enc2h.at[k, d], recv2h.at[k, d], r2h_s.at[k, d], r2h_r.at[k, d], dev_y[d]))
        return got

    def c_ag1(k):
        ref = full.at[k, 1, my_rows, full_cols_of(y)]
        got = [remote(ref, ref, a1g_s.at[k], a1g_r.at[k], dev_x)]
        ref = full.at[k, 0, my_rows, full_cols_of(y)]
        for d in (1, 0, 2):
            got.append(remote(ref, ref, a1h_s.at[k, d], a1h_r.at[k, d], dev_y[d]))
        return got

    def c_ag2(k):
        ref = full.at[k, 0, my_rows, my_half]
        got = [remote(ref, ref, a2h_s.at[k], a2h_r.at[k], dev_x)]
        ref = full.at[k, 1, :, full_cols_of(y)]
        for d in (1, 0, 2):
            got.append(remote(ref, ref, a2g_s.at[k, d], a2g_r.at[k, d], dev_y[d]))
        return got

    def c_share(k):
        ref = full.at[k, :, :, my_half]
        return [remote(ref, ref, cs_s.at[k], cs_r.at[k], dev_core)]

    def c_out(k, ds):
        return [
            remote(out_s.at[k, d - 1], out_r.at[k, d - 1], on_s.at[k, d - 1], on_r.at[k, d - 1], dev_z[d]) for d in ds
        ]

    def c_out_far(k):
        got = []
        for i, d in enumerate((1, NZ - 1)):
            rows = pl.ds(16 * i, 16)
            got.append(
                remote(far_s.at[k, rows, :], far_r.at[k, rows, :], of_s.at[k, i], of_r.at[k, i], dev_z[d])
            )
        return got

    def c_xout(k):
        return [remote(xs.at[k], xr.at[k], xo_s.at[k], xo_r.at[k], dev_xh)]

    def start(copies):
        for c in copies:
            c.start()

    def received(copies):
        for c in copies:
            c.wait_recv()

    def sent(copies):
        for c in copies:
            c.wait_send()

    def z_start(k):
        start(c_near(k))

    def z_pass(k):
        received(c_near(k, NEAR[:2]))
        start(c_far(k))

    def z_end(k):
        received(c_near(k, NEAR[2:]))
        received(c_far(k))

    def build_unit(k):
        a = own[k].astype(F32)
        b = part[k].astype(F32)

        def joined(v, r):
            return jnp.concatenate([v[r : r + 8], v[r + 8 : r + 16]], axis=1)

        first = xh == 0
        pieces = []
        for r in (0, 16):
            m, o = joined(a, r), joined(b, r)
            pieces += [jnp.where(first, m, o), jnp.where(first, o, m)]
        unit[k, z] = jnp.concatenate(pieces, axis=0).astype(BF16)

    def first_products(k):
        xin = unit[k, :, 0:16, :].reshape(M, D)
        gin_ = unit[k, :, 16:32, :].reshape(M, D)
        step = 512
        for j in range(0, HF, step):
            at = pl.ds(pl.multiple_of(other_base + j, 128), step)
            half_s[k, 0, :, j : j + step] = coded(times(xin, w1[:, at]))
        for j in range(0, HF, step):
            at = pl.ds(pl.multiple_of(other_base + j, 128), step)
            half_s[k, 1, :, j : j + step] = coded(times_transposed(gin_, w2[at, :]))
        start(c_core(k))
        for j in range(0, HF, step):
            at = pl.ds(pl.multiple_of(base + j, 128), step)
            sum_f[k, 0, :, j : j + step] = times(xin, w1[:, at])
        for j in range(0, HF, step):
            at = pl.ds(pl.multiple_of(base + j, 128), step)
            sum_f[k, 1, :, j : j + step] = times_transposed(gin_, w2[at, :])

    def reduce_first(k):
        received(c_core(k))
        enc1[k, 0, other_rows, :] = coded(sum_f[k, 0, other_rows, :] + decoded(half_r[k, 0, other_rows, :]))
        for d in range(NY - 1):
            at = cols_of(y_of[d])
            enc1[k, 1, :, at] = coded(sum_f[k, 1, :, at] + decoded(half_r[k, 1, :, at]))
        start(c_rs1(k))
        sum_f[k, 0, my_rows, :] = sum_f[k, 0, my_rows, :] + decoded(half_r[k, 0, my_rows, :])
        at = cols_of(y)
        sum_f[k, 1, :, at] = sum_f[k, 1, :, at] + decoded(half_r[k, 1, :, at])

    def reduce_second(k):
        received(c_rs1(k))
        for d in range(NY - 1):
            at = cols_of(y_of[d])
            enc2h[k, d] = coded(sum_f[k, 0, my_rows, at] + decoded(recv1h[k, :, at]))
        at = cols_of(y)

        def total(rows):
            got = sum_f[k, 1, rows, at]
            for d in range(NY - 1):
                got = got + decoded(recv1g[k, d, rows, :])
            return got

        enc2g[k] = coded(total(other_rows))
        start(c_rs2(k))
        keep2h[k] = sum_f[k, 0, my_rows, at] + decoded(recv1h[k, :, at])
        keep2g[k] = total(my_rows)

    def activate(k):
        received(c_rs2(k))
        h = keep2h[k]
        for d in range(NY - 1):
            h = h + decoded(recv2h[k, d])
        g = keep2g[k] + decoded(recv2g[k])
        t = jnp.tanh(coef_a * (h + coef_b * h * h * h))
        act = 0.5 * h * (1.0 + t)
        slope = 0.5 * (1.0 + t) + 0.5 * h * (1.0 - t * t) * coef_a * (1.0 + 3.0 * coef_b * h * h)
        full[k, 0, my_rows, full_cols_of(y)] = act.astype(BF16)
        full[k, 1, my_rows, full_cols_of(y)] = (g * slope).astype(BF16)
        start(c_ag1(k))

    def gather_second(k):
        received(c_ag1(k))
        start(c_ag2(k))

    def gather_third(k):
        received(c_ag2(k))
        start(c_share(k))

    def own_out(k, b):
        return ot[k % 3, :, b].reshape(32, D)

    def out_first(k):
        v = own_out(k, (z + 4) % NZ)
        far_s[k] = coded(v, LIFT_OUT)
        start(c_out_far(k))
        for d in (2, 6, 1, 7):
            out_s[k, d - 1] = coded(own_out(k, (z + d) % NZ), LIFT_OUT)
            start(c_out(k, (d,)))

    def out_second(k):
        c = c_out_far(k)
        received(c[:1])
        v = own_out(k, (z + 3) % NZ)
        out_s[k, 2, 0:16, :] = coded(v[0:16] + decoded(far_r[k, 0:16, :], LIFT_OUT), LIFT_OUT)
        out_s[k, 2, 16:32, :] = coded(v[16:32], LIFT_OUT)
        start(c_out(k, (3,)))
        received(c[1:])
        v = own_out(k, (z + 5) % NZ)
        out_s[k, 4, 0:16, :] = coded(v[0:16], LIFT_OUT)
        out_s[k, 4, 16:32, :] = coded(v[16:32] + decoded(far_r[k, 16:32, :], LIFT_OUT), LIFT_OUT)
        start(c_out(k, (5,)))

    def second_products(k):
        received(c_share(k))
        ot[k % 3, 0] = times(full[k, 0], w2[...]).reshape(NZ, 16, D)
        ot[k % 3, 1] = times_transposed(full[k, 1], w1[...]).reshape(NZ, 16, D)
        out_first(k)

    def reduce_out(k):
        received(c_out(k, NEAR))
        total = own_out(k, z)
        for d in NEAR:
            total = total + decoded(out_r[k, d - 1], LIFT_OUT)
        first = xh == 0
        for i in range(2):
            lo, hi = total[16 * i : 16 * i + 8], total[16 * i + 8 : 16 * i + 16]
            mine[k, 8 * i : 8 * i + 8, :] = jnp.where(first, lo, hi)
            xs[k, 8 * i : 8 * i + 8, :] = jnp.where(first, hi, lo)
        start(c_xout(k))

    def finish(k):
        received(c_xout(k))
        at = pl.ds(pl.multiple_of(8 * k, 8), 8)
        out[at, :] = mine[k, 0:8, :] + xr[k, 0:8, :]
        gin[at, :] = mine[k, 8:16, :] + xr[k, 8:16, :]

    cw1 = pltpu.make_async_copy(w1_hbm, w1, wsem.at[0])
    cw2 = pltpu.make_async_copy(w2_hbm, w2, wsem.at[1])
    cw1.start()
    cw2.start()
    peers = [dev_core, dev_x, dev_xh] + dev_y + [dev_z[d] for d in NEAR]
    barrier = pltpu.get_barrier_semaphore()
    for p in peers:
        pl.semaphore_signal(barrier, inc=1, device_id=p, device_id_type=MESH)
    a = inp[...].astype(F32)
    g = gout[...].astype(F32)
    hd = D // 2
    for k in range(T):
        s = slice(8 * k, 8 * k + 8)
        own[k] = jnp.concatenate([a[s, :hd], a[s, hd:], g[s, :hd], g[s, hd:]], axis=0).astype(BF16)
    pl.semaphore_wait(barrier, len(peers))
    for k in range(T):
        start(c_part(k))
    received(c_part(0))
    build_unit(0)
    z_start(0)
    for k in range(1, T):
        received(c_part(k))
        build_unit(k)
    z_pass(0)
    z_start(1)
    cw1.wait()
    cw2.wait()

    def step(t, carry):
        def when(k, body):
            @pl.when(jnp.logical_and(k >= 0, k < T))
            def _():
                body(k)

        when(t - 1, activate)
        when(t, reduce_second)
        when(t - 2, gather_second)
        when(t + 1, reduce_first)
        when(t - 3, gather_third)
        when(t - 4, out_second)
        when(t + 2, z_end)
        when(t + 2, first_products)
        when(t - 5, finish)
        when(t - 3, second_products)
        when(t - 4, reduce_out)

        @pl.when(jnp.logical_and(t + 3 >= 1, t + 3 < T))
        def _():
            z_pass(t + 3)

        @pl.when(jnp.logical_and(t + 4 >= 2, t + 4 < T))
        def _():
            z_start(t + 4)

        return carry

    lax.fori_loop(-2, T + 3, step, 0)

    def drain(k, carry):
        for copies in (c_part, c_core, c_rs1, c_rs2, c_ag1, c_ag2, c_share):
            sent(copies(k))
        sent(c_near(k))
        sent(c_far(k))
        return carry

    def drain_out(k, carry):
        sent(c_out_far(k))
        sent(c_out(k, NEAR))
        sent(c_xout(k))
        return carry

    last = T - 1
    out_second(last)
    finish(last - 1)
    lax.fori_loop(0, T, drain, 0)
    lax.fori_loop(0, last, drain_out, 0)
    reduce_out(last)
    finish(last)
    drain_out(last, 0)


def hand_over(a, b, out, gin):
    out[...] = a[...]
    gin[...] = b[...]


def on_device(inputs, w_first, w_second, grad_out):
    tokens, D = inputs.shape
    FF = w_first.shape[1]
    T = tokens // 8
    M = 16 * NZ
    HM, HF = M // 2, FF // 2
    QF = HF // NY
    V = pl.BlockSpec(memory_space=pltpu.VMEM)
    ANY = pl.BlockSpec(memory_space=pl.ANY)
    shape = jax.ShapeDtypeStruct((tokens, D), F32)
    dma = pltpu.SemaphoreType.DMA
    one, three = dma((T,)), dma((T, NY - 1))
    buffers = [
        pltpu.VMEM((D, FF), BF16),
        pltpu.VMEM((FF, D), BF16),
        pltpu.VMEM((T, 32, D // 2), BF16),
        pltpu.VMEM((T, 32, D // 2), BF16),
        pltpu.VMEM((T, NZ, 32, D), BF16),
        pltpu.VMEM((T, 2, M, HF), F32),
        pltpu.VMEM((T, 2, M, HF), BF16),
        pltpu.VMEM((T, 2, M, HF), BF16),
        pltpu.VMEM((T, 2, M, HF), BF16),
        pltpu.VMEM((T, HM, HF), BF16),
        pltpu.VMEM((T, NY - 1, M, QF), BF16),
        pltpu.VMEM((T, NY - 1, HM, QF), BF16),
        pltpu.VMEM((T, HM, QF), BF16),
        pltpu.VMEM((T, HM, QF), F32),
        pltpu.VMEM((T, HM, QF), F32),
        pltpu.VMEM((T, NY - 1, HM, QF), BF16),
        pltpu.VMEM((T, HM, QF), BF16),
        pltpu.VMEM((T, 2, M, FF), BF16),
        pltpu.VMEM((T, NZ - 1, 32, D), BF16),
        pltpu.VMEM((T, NZ - 1, 32, D), BF16),
        pltpu.VMEM((T, 32, D), BF16),
        pltpu.VMEM((T, 32, D), BF16),
        pltpu.VMEM((3, 2, NZ, 16, D), F32),
        pltpu.VMEM((T, 16, D), F32),
        pltpu.VMEM((T, 16, D), F32),
        pltpu.VMEM((T, 16, D), F32),
    ]
    semaphores = [
        dma((2,)),
        one, one,
        dma((T, NZ - 1)), dma((T, NZ - 1)), dma((T, 2)), dma((T, 2)),
        one, one,
        one, one, three, three,
        three, three, one, one,
        three, three, one, one,
        one, one, three, three,
        one, one,
        dma((T, NZ - 1)), dma((T, NZ - 1)), dma((T, 2)), dma((T, 2)),
        one, one,
    ]
    flops = 4 * 2 * M * T * D * FF
    parts = pl.pallas_call(
        functools.partial(kernel, T),
        out_shape=(shape, shape),
        in_specs=[V, ANY, ANY, V],
        out_specs=(V, V),
        scratch_shapes=buffers + semaphores,
        compiler_params=pltpu.CompilerParams(
            collective_id=0, has_side_effects=True, vmem_limit_bytes=63 * 2**20
        ),
        cost_estimate=pl.CostEstimate(flops=flops, bytes_accessed=4 * D * FF, transcendentals=0),
    )(inputs, w_first, w_second, grad_out)
    return pl.pallas_call(hand_over, out_shape=(shape, shape), in_specs=[V, V], out_specs=(V, V))(*parts)


def solution(mesh):
    in_specs = (P("col", "row"), P("row", "col"), P("col", "row"), P("col", "row"))
    out_specs = (P("col", "row"), P("col", "row"))
    return jax.shard_map(
        on_device, mesh=mesh, in_specs=in_specs, out_specs=out_specs, check_vma=False
    )
```

```python
import functools

import jax
import jax.numpy as jnp
from jax import lax
from jax.experimental import pallas as pl
from jax.experimental.pallas import tpu as pltpu
from jax.sharding import PartitionSpec as P

MESH = pl.DeviceIdType.MESH
F32 = jnp.float32
BF16 = jnp.bfloat16

coef_a = 0.7978845608
coef_b = 0.044715

NY, NZ = 4, 8
NEAR = (3, 5, 2, 6, 1, 7)
LIFT = 2.0**19
LIFT_OUT = 2.0**8


def times(panel, weight):
    return jnp.dot(panel, weight, preferred_element_type=F32)


def times_transposed(panel, weight):
    return lax.dot_general(panel, weight, (((1,), (1,)), ((), ())), preferred_element_type=F32)


def coded(v, lift=LIFT):
    v = v * lift
    w = v * v
    w = w * w
    return jnp.where(v < 0, -w, w).astype(BF16)


def decoded(c, lift=LIFT):
    w = c.astype(F32)
    v = lax.rsqrt(lax.rsqrt(jnp.abs(w))) * (1.0 / lift)
    return jnp.where(w < 0, -v, v)


def kernel(
    T, inp, w1_hbm, w2_hbm, gout, out, gin,
    w1, w2, own, part, unit, sum_f, half_s, half_r, enc1, recv1h, recv1g, enc2h, enc2g, keep2h, keep2g,
    recv2h, recv2g, full, out_s, out_r, far_s, far_r, ot, mine, xs, xr,
    wsem, part_s, part_r, zn_s, zn_r, zf_s, zf_r, core_s, core_r, r1h_s, r1h_r, r1g_s, r1g_r,
    r2h_s, r2h_r, r2g_s, r2g_r, a1h_s, a1h_r, a1g_s, a1g_r, a2h_s, a2h_r, a2g_s, a2g_r,
    cs_s, cs_r, on_s, on_r, of_s, of_r, xo_s, xo_r,
):
    row = lax.axis_index("row")
    col = lax.axis_index("col")
    xl, y, core = row // 8, (row // 2) % NY, row % 2
    z, xh = col // 2, col % 2
    D = w1.shape[0]
    FF = w1.shape[1]
    HF = FF // 2
    QF = HF // NY
    M = 16 * NZ
    HM = M // 2

    def at_row(a, b, c):
        return (a * 8 + b * 2 + c, col)

    def at_col(a, b):
        return (row, a * 2 + b)

    dev_core = at_row(xl, y, 1 - core)
    dev_x = at_row(1 - xl, y, core)
    dev_y = [at_row(xl, (y + d) % NY, core) for d in range(1, NY)]
    dev_z = [at_col((z + d) % NZ, xh) for d in range(NZ)]
    dev_xh = at_col(z, 1 - xh)

    def remote(src, dst, ss, rs, dev):
        return pltpu.make_async_remote_copy(
            src_ref=src, dst_ref=dst, send_sem=ss, recv_sem=rs, device_id=dev, device_id_type=MESH
        )

    my_rows = pl.ds(pl.multiple_of(xl * HM, HM), HM)
    other_rows = pl.ds(pl.multiple_of((1 - xl) * HM, HM), HM)
    base = core * HF
    other_base = (1 - core) * HF

    def cols_of(q):
        return pl.ds(pl.multiple_of(q * QF, 128), QF)

    def full_cols_of(q):
        return pl.ds(pl.multiple_of(base + q * QF, 128), QF)

    my_half = pl.ds(pl.multiple_of(base, 128), HF)
    y_of = [(y + d) % NY for d in range(1, NY)]

    def c_part(k):
        return [remote(own.at[k], part.at[k], part_s.at[k], part_r.at[k], dev_xh)]

    def c_near(k, ds=NEAR):
        ref = unit.at[k, z]
        return [remote(ref, ref, zn_s.at[k, d - 1], zn_r.at[k, d - 1], dev_z[d]) for d in ds]

    def c_far(k):
        got = []
        for i, (b, d) in enumerate(((NZ - 3, 1), (3, NZ - 1))):
            ref = unit.at[k, (z + b) % NZ, pl.ds(16 * i, 16), :]
            got.append(remote(ref, ref, zf_s.at[k, i], zf_r.at[k, i], dev_z[d]))
        return got

    def c_core(k):
        return [remote(half_s.at[k], half_r.at[k], core_s.at[k], core_r.at[k], dev_core)]

    def c_rs1(k):
        got = [remote(enc1.at[k, 0, other_rows, :], recv1h.at[k], r1h_s.at[k], r1h_r.at[k], dev_x)]
        for d in (1, 0, 2):
            got.append(
                remote(
                    enc1.at[k, 1, :, cols_of(y_of[d])], recv1g.at[k, d], r1g_s.at[k, d], r1g_r.at[k, d], dev_y[d]
                )
            )
        return got

    def c_rs2(k):
        got = [remote(enc2g.at[k], recv2g.at[k], r2g_s.at[k], r2g_r.at[k], dev_x)]
        for d in (1, 0, 2):
            got.append(remote(enc2h.at[k, d], recv2h.at[k, d], r2h_s.at[k, d], r2h_r.at[k, d], dev_y[d]))
        return got

    def c_ag1(k):
        ref = full.at[k, 1, my_rows, full_cols_of(y)]
        got = [remote(ref, ref, a1g_s.at[k], a1g_r.at[k], dev_x)]
        ref = full.at[k, 0, my_rows, full_cols_of(y)]
        for d in (1, 0, 2):
            got.append(remote(ref, ref, a1h_s.at[k, d], a1h_r.at[k, d], dev_y[d]))
        return got

    def c_ag2(k):
        ref = full.at[k, 0, my_rows, my_half]
        got = [remote(ref, ref, a2h_s.at[k], a2h_r.at[k], dev_x)]
        ref = full.at[k, 1, :, full_cols_of(y)]
        for d in (1, 0, 2):
            got.append(remote(ref, ref, a2g_s.at[k, d], a2g_r.at[k, d], dev_y[d]))
        return got

    def c_share(k):
        refs = [full.at[k, i, :, my_half] for i in range(2)]
        return [remote(r, r, cs_s.at[k, i], cs_r.at[k, i], dev_core) for i, r in enumerate(refs)]

    def c_out(k, ds):
        return [
            remote(out_s.at[k, d - 1], out_r.at[k, d - 1], on_s.at[k, d - 1], on_r.at[k, d - 1], dev_z[d]) for d in ds
        ]

    def c_out_far(k):
        got = []
        for i, d in enumerate((1, NZ - 1)):
            rows = pl.ds(16 * i, 16)
            got.append(
                remote(far_s.at[k, rows, :], far_r.at[k, rows, :], of_s.at[k, i], of_r.at[k, i], dev_z[d])
            )
        return got

    def c_xout(k):
        return [remote(xs.at[k], xr.at[k], xo_s.at[k], xo_r.at[k], dev_xh)]

    def start(copies):
        for c in copies:
            c.start()

    def received(copies):
        for c in copies:
            c.wait_recv()

    def sent(copies):
        for c in copies:
            c.wait_send()

    def z_start(k):
        start(c_near(k))

    def z_pass(k):
        received(c_near(k, NEAR[:2]))
        start(c_far(k))

    def z_end(k):
        received(c_near(k, NEAR[2:]))
        received(c_far(k))

    def build_unit(k):
        a = own[k].astype(F32)
        b = part[k].astype(F32)

        def joined(v, r):
            return jnp.concatenate([v[r : r + 8], v[r + 8 : r + 16]], axis=1)

        first = xh == 0
        pieces = []
        for r in (0, 16):
            m, o = joined(a, r), joined(b, r)
            pieces += [jnp.where(first, m, o), jnp.where(first, o, m)]
        unit[k, z] = jnp.concatenate(pieces, axis=0).astype(BF16)

    def first_products(k):
        xin = unit[k, :, 0:16, :].reshape(M, D)
        gin_ = unit[k, :, 16:32, :].reshape(M, D)
        step = 512
        for j in range(0, HF, step):
            at = pl.ds(pl.multiple_of(other_base + j, 128), step)
            half_s[k, 0, :, j : j + step] = coded(times(xin, w1[:, at]))
        for j in range(0, HF, step):
            at = pl.ds(pl.multiple_of(other_base + j, 128), step)
            half_s[k, 1, :, j : j + step] = coded(times_transposed(gin_, w2[at, :]))
        start(c_core(k))
        for j in range(0, HF, step):
            at = pl.ds(pl.multiple_of(base + j, 128), step)
            sum_f[k, 0, :, j : j + step] = times(xin, w1[:, at])
        for j in range(0, HF, step):
            at = pl.ds(pl.multiple_of(base + j, 128), step)
            sum_f[k, 1, :, j : j + step] = times_transposed(gin_, w2[at, :])

    def reduce_first(k):
        received(c_core(k))
        enc1[k, 0, other_rows, :] = coded(sum_f[k, 0, other_rows, :] + decoded(half_r[k, 0, other_rows, :]))
        for d in range(NY - 1):
            at = cols_of(y_of[d])
            enc1[k, 1, :, at] = coded(sum_f[k, 1, :, at] + decoded(half_r[k, 1, :, at]))
        start(c_rs1(k))
        sum_f[k, 0, my_rows, :] = sum_f[k, 0, my_rows, :] + decoded(half_r[k, 0, my_rows, :])
        at = cols_of(y)
        sum_f[k, 1, :, at] = sum_f[k, 1, :, at] + decoded(half_r[k, 1, :, at])

    def reduce_second(k):
        received(c_rs1(k))
        for d in range(NY - 1):
            at = cols_of(y_of[d])
            enc2h[k, d] = coded(sum_f[k, 0, my_rows, at] + decoded(recv1h[k, :, at]))
        at = cols_of(y)

        def total(rows):
            got = sum_f[k, 1, rows, at]
            for d in range(NY - 1):
                got = got + decoded(recv1g[k, d, rows, :])
            return got

        enc2g[k] = coded(total(other_rows))
        start(c_rs2(k))
        keep2h[k] = sum_f[k, 0, my_rows, at] + decoded(recv1h[k, :, at])
        keep2g[k] = total(my_rows)

    def activate(k):
        received(c_rs2(k))
        h = keep2h[k]
        for d in range(NY - 1):
            h = h + decoded(recv2h[k, d])
        g = keep2g[k] + decoded(recv2g[k])
        t = jnp.tanh(coef_a * (h + coef_b * h * h * h))
        act = 0.5 * h * (1.0 + t)
        slope = 0.5 * (1.0 + t) + 0.5 * h * (1.0 - t * t) * coef_a * (1.0 + 3.0 * coef_b * h * h)
        full[k, 0, my_rows, full_cols_of(y)] = act.astype(BF16)
        full[k, 1, my_rows, full_cols_of(y)] = (g * slope).astype(BF16)
        start(c_ag1(k))

    def gather_second(k):
        received(c_ag1(k))
        start(c_ag2(k))

    def gather_third(k):
        received(c_ag2(k))
        start(c_share(k))

    def own_out(k, b):
        return ot[k % 3, :, b].reshape(32, D)

    def out_first(k):
        v = own_out(k, (z + 4) % NZ)
        far_s[k] = coded(v, LIFT_OUT)
        start(c_out_far(k))
        for d in (2, 6, 1, 7):
            out_s[k, d - 1] = coded(own_out(k, (z + d) % NZ), LIFT_OUT)
            start(c_out(k, (d,)))

    def out_second(k):
        c = c_out_far(k)
        received(c[:1])
        v = own_out(k, (z + 3) % NZ)
        out_s[k, 2, 0:16, :] = coded(v[0:16] + decoded(far_r[k, 0:16, :], LIFT_OUT), LIFT_OUT)
        out_s[k, 2, 16:32, :] = coded(v[16:32], LIFT_OUT)
        start(c_out(k, (3,)))
        received(c[1:])
        v = own_out(k, (z + 5) % NZ)
        out_s[k, 4, 0:16, :] = coded(v[0:16], LIFT_OUT)
        out_s[k, 4, 16:32, :] = coded(v[16:32] + decoded(far_r[k, 16:32, :], LIFT_OUT), LIFT_OUT)
        start(c_out(k, (5,)))

    def second_products(k):
        share = c_share(k)
        received(share[:1])
        ot[k % 3, 0] = times(full[k, 0], w2[...]).reshape(NZ, 16, D)
        received(share[1:])
        ot[k % 3, 1] = times_transposed(full[k, 1], w1[...]).reshape(NZ, 16, D)
        out_first(k)

    def reduce_out(k):
        received(c_out(k, NEAR))
        total = own_out(k, z)
        for d in NEAR:
            total = total + decoded(out_r[k, d - 1], LIFT_OUT)
        first = xh == 0
        for i in range(2):
            lo, hi = total[16 * i : 16 * i + 8], total[16 * i + 8 : 16 * i + 16]
            mine[k, 8 * i : 8 * i + 8, :] = jnp.where(first, lo, hi)
            xs[k, 8 * i : 8 * i + 8, :] = jnp.where(first, hi, lo)
        start(c_xout(k))

    def finish(k):
        received(c_xout(k))
        at = pl.ds(pl.multiple_of(8 * k, 8), 8)
        out[at, :] = mine[k, 0:8, :] + xr[k, 0:8, :]
        gin[at, :] = mine[k, 8:16, :] + xr[k, 8:16, :]

    cw1 = pltpu.make_async_copy(w1_hbm, w1, wsem.at[0])
    cw2 = pltpu.make_async_copy(w2_hbm, w2, wsem.at[1])
    cw1.start()
    cw2.start()
    peers = [dev_core, dev_x, dev_xh] + dev_y + [dev_z[d] for d in NEAR]
    barrier = pltpu.get_barrier_semaphore()
    for p in peers:
        pl.semaphore_signal(barrier, inc=1, device_id=p, device_id_type=MESH)
    a = inp[...].astype(F32)
    g = gout[...].astype(F32)
    hd = D // 2
    for k in range(T):
        s = slice(8 * k, 8 * k + 8)
        own[k] = jnp.concatenate([a[s, :hd], a[s, hd:], g[s, :hd], g[s, hd:]], axis=0).astype(BF16)
    pl.semaphore_wait(barrier, len(peers))
    for k in range(T):
        start(c_part(k))
    received(c_part(0))
    build_unit(0)
    z_start(0)
    for k in range(1, T):
        received(c_part(k))
        build_unit(k)
    z_pass(0)
    z_start(1)
    cw1.wait()
    cw2.wait()

    def step(t, carry):
        def when(k, body):
            @pl.when(jnp.logical_and(k >= 0, k < T))
            def _():
                body(k)

        when(t - 1, activate)
        when(t, reduce_second)
        when(t - 2, gather_second)
        when(t + 1, reduce_first)
        when(t - 3, gather_third)
        when(t - 4, out_second)
        when(t + 2, z_end)
        when(t + 2, first_products)
        when(t - 5, finish)
        when(t - 3, second_products)
        when(t - 4, reduce_out)

        @pl.when(jnp.logical_and(t + 3 >= 1, t + 3 < T))
        def _():
            z_pass(t + 3)

        @pl.when(jnp.logical_and(t + 4 >= 2, t + 4 < T))
        def _():
            z_start(t + 4)

        return carry

    lax.fori_loop(-2, T + 3, step, 0)

    def drain(k, carry):
        for copies in (c_part, c_core, c_rs1, c_rs2, c_ag1, c_ag2, c_share):
            sent(copies(k))
        sent(c_near(k))
        sent(c_far(k))
        return carry

    def drain_out(k, carry):
        sent(c_out_far(k))
        sent(c_out(k, NEAR))
        sent(c_xout(k))
        return carry

    last = T - 1
    out_second(last)
    finish(last - 1)
    lax.fori_loop(0, T, drain, 0)
    lax.fori_loop(0, last, drain_out, 0)
    reduce_out(last)
    finish(last)
    drain_out(last, 0)


def hand_over(a, b, out, gin):
    out[...] = a[...]
    gin[...] = b[...]


def on_device(inputs, w_first, w_second, grad_out):
    tokens, D = inputs.shape
    FF = w_first.shape[1]
    T = tokens // 8
    M = 16 * NZ
    HM, HF = M // 2, FF // 2
    QF = HF // NY
    V = pl.BlockSpec(memory_space=pltpu.VMEM)
    ANY = pl.BlockSpec(memory_space=pl.ANY)
    shape = jax.ShapeDtypeStruct((tokens, D), F32)
    dma = pltpu.SemaphoreType.DMA
    one, three = dma((T,)), dma((T, NY - 1))
    buffers = [
        pltpu.VMEM((D, FF), BF16),
        pltpu.VMEM((FF, D), BF16),
        pltpu.VMEM((T, 32, D // 2), BF16),
        pltpu.VMEM((T, 32, D // 2), BF16),
        pltpu.VMEM((T, NZ, 32, D), BF16),
        pltpu.VMEM((T, 2, M, HF), F32),
        pltpu.VMEM((T, 2, M, HF), BF16),
        pltpu.VMEM((T, 2, M, HF), BF16),
        pltpu.VMEM((T, 2, M, HF), BF16),
        pltpu.VMEM((T, HM, HF), BF16),
        pltpu.VMEM((T, NY - 1, M, QF), BF16),
        pltpu.VMEM((T, NY - 1, HM, QF), BF16),
        pltpu.VMEM((T, HM, QF), BF16),
        pltpu.VMEM((T, HM, QF), F32),
        pltpu.VMEM((T, HM, QF), F32),
        pltpu.VMEM((T, NY - 1, HM, QF), BF16),
        pltpu.VMEM((T, HM, QF), BF16),
        pltpu.VMEM((T, 2, M, FF), BF16),
        pltpu.VMEM((T, NZ - 1, 32, D), BF16),
        pltpu.VMEM((T, NZ - 1, 32, D), BF16),
        pltpu.VMEM((T, 32, D), BF16),
        pltpu.VMEM((T, 32, D), BF16),
        pltpu.VMEM((3, 2, NZ, 16, D), F32),
        pltpu.VMEM((T, 16, D), F32),
        pltpu.VMEM((T, 16, D), F32),
        pltpu.VMEM((T, 16, D), F32),
    ]
    semaphores = [
        dma((2,)),
        one, one,
        dma((T, NZ - 1)), dma((T, NZ - 1)), dma((T, 2)), dma((T, 2)),
        one, one,
        one, one, three, three,
        three, three, one, one,
        three, three, one, one,
        one, one, three, three,
        dma((T, 2)), dma((T, 2)),
        dma((T, NZ - 1)), dma((T, NZ - 1)), dma((T, 2)), dma((T, 2)),
        one, one,
    ]
    flops = 4 * 2 * M * T * D * FF
    parts = pl.pallas_call(
        functools.partial(kernel, T),
        out_shape=(shape, shape),
        in_specs=[V, ANY, ANY, V],
        out_specs=(V, V),
        scratch_shapes=buffers + semaphores,
        compiler_params=pltpu.CompilerParams(
            collective_id=0, has_side_effects=True, vmem_limit_bytes=63 * 2**20
        ),
        cost_estimate=pl.CostEstimate(flops=flops, bytes_accessed=4 * D * FF, transcendentals=0),
    )(inputs, w_first, w_second, grad_out)
    return pl.pallas_call(hand_over, out_shape=(shape, shape), in_specs=[V, V], out_specs=(V, V))(*parts)


def solution(mesh):
    in_specs = (P("col", "row"), P("row", "col"), P("col", "row"), P("col", "row"))
    out_specs = (P("col", "row"), P("col", "row"))
    return jax.shard_map(
        on_device, mesh=mesh, in_specs=in_specs, out_specs=out_specs, check_vma=False
    )
```
